32 devices in a mesh: pool: 16 (over z, x, core), exp: 2 (over y).
Axes of the slice: x: 2, y: 2, z: 4, core: 2. Of those that a mesh axis runs over, the one named last changes fastest.
Arguments:
- tokens: bfloat16 [256, 1024], P('pool'), as said below
- block_table: int32 [256, 128], replicated, may hold values from -1 to 2303, as said below
- lengths: int32 [256], replicated, may hold values from 1 to 16384, as said below
- k_cache: bfloat16 [2048, 128, 512], P('pool', None, 'exp'), as said below
- v_cache: bfloat16 [2048, 128, 512], P('pool', None, 'exp'), may hold values from -9 to 9
- hidden_store: bfloat16 [256, 128, 1024], P('pool'), may hold values from -6 to 6
- norm_attn: bfloat16 [1024], replicated, may hold values from 0.5 to 1.5
- w_query: bfloat16 [1024, 1024], P(None, 'exp'), as said below
- w_key: bfloat16 [1024, 512], P(None, 'exp'), may hold values from -0.1875 to 0.1875
- w_value: bfloat16 [1024, 512], P(None, 'exp'), may hold values from -0.1875 to 0.1875
- w_out: bfloat16 [1024, 1024], P('exp'), may hold values from -0.1875 to 0.1875
- norm_moe: bfloat16 [1024], replicated, may hold values from 0.5 to 1.5
- expert_ids: int32 [256, 8], P('pool'), may hold values from 0 to 15, all different within a row; in each aligned block of 16 rows (0 to 15, 16 to 31, ...) at most 16 rows name the same one
- gate_weights: float32 [256, 8], P('pool'), may hold values from 0.1 to 1
- w_gate: bfloat16 [16, 1024, 512], P('pool'), may hold values from -0.1875 to 0.1875
- w_up: bfloat16 [16, 1024, 512], P('pool'), may hold values from -0.1875 to 0.1875
- w_down: bfloat16 [16, 512, 1024], P('pool'), may hold values from -0.25 to 0.25
Outputs:
- layer_out: bfloat16 [256, 1024], P('pool', 'exp')
The draws below stay inside these ranges and needn't reach their ends.
Inputs may be any that keep to these rules, and one draw needn't show every extreme that they name: `block_table`: every block number 0 to 2303 stands exactly once in the table; a request's blocks fill the start of its row and -1 fills the rest; each request has 1 to 128 blocks and some request has exactly 128. `lengths`: A request with n blocks has a length above (n - 1) * 128 and at most n * 128; some request has the length 16384. `expert_ids`: in the rows of one pool index no expert is named by more than 16 rows. `tokens`: entries lie within -8 to 8. `k_cache`: entries lie within -8 to 8. `w_query`: entries are of magnitude below 7 / sqrt(1024).
All inputs are finite; a program needn't handle non-finite values.
Results may differ from the reference program's by a relative error of at most 0.009.
Values may be sent and summed in bfloat16 or wider, within the bound.
A program may use at most 128 MiB of HBM per device.

```python
import math
import jax
import jax.numpy as jnp
import numpy as np
from jax import lax

D = 1024
QUERY_HEADS = 16
KEY_VALUE_HEADS = 8
HEAD_SIZE = 64
FF = 512
TOP = 8
BLOCK_TOKENS = 128
REQUEST_BLOCKS = 128
REQ_DEV = 16
NB_DEV = 128
NH_DEV = 16
TOTAL_SLOTS = 2304
KV_BLOCKS = 2048
HIDDEN_BLOCKS = 256
REQUESTS = 256
EXPERTS = 16
CAP = 16
QW = 1024
KW = 512
N_POOL = 16


def table_parts(key):
    base_key = jax.random.fold_in(key, 14)
    key_heavy, key_weight, key_order, key_perm, key_tail = jax.random.split(base_key, 5)
    req_ids = jnp.arange(REQUESTS, dtype=jnp.int32)
    heavy_req = jax.random.randint(key_heavy, (), 0, REQUESTS)
    heavy_flag = req_ids == heavy_req
    draw_weight = jax.random.randint(key_weight, (REQUESTS,), 1, 3) ** 2
    draw_weight = jnp.where(heavy_flag, 0, draw_weight)
    extra_blocks = TOTAL_SLOTS - REQUEST_BLOCKS - (REQUESTS - 1)
    shared_block_list = extra_blocks * draw_weight // jnp.sum(draw_weight)
    remaining_count = extra_blocks - jnp.sum(shared_block_list)
    order_perm = jax.random.permutation(key_order, REQUESTS)
    req_rank = jnp.zeros((REQUESTS,), jnp.int32).at[order_perm].set(req_ids)
    heavy_rank = req_rank[heavy_req]
    peer_rank = req_rank - jnp.where(req_rank > heavy_rank, 1, 0)
    extra_credit = jnp.where((peer_rank < remaining_count) & jnp.logical_not(heavy_flag), 1, 0)
    token_counts = jnp.where(heavy_flag, REQUEST_BLOCKS, 1 + shared_block_list + extra_credit).astype(jnp.int32)
    offsets = jnp.cumsum(token_counts) - token_counts
    slot_perm = jax.random.permutation(key_perm, TOTAL_SLOTS).astype(jnp.int32)
    list_pos = jnp.arange(REQUEST_BLOCKS, dtype=jnp.int32)
    gather_at = jnp.clip(offsets[:, None] + list_pos[None, :], 0, TOTAL_SLOTS - 1)
    table = jnp.where(list_pos[None, :] < token_counts[:, None], slot_perm[gather_at], -1)
    tail_len = jax.random.randint(key_tail, (REQUESTS,), 1, BLOCK_TOKENS + 1)
    tail_len = jnp.where(heavy_flag, BLOCK_TOKENS, tail_len)
    length_vals = (token_counts - 1) * BLOCK_TOKENS + tail_len
    return (table.astype(jnp.int32), length_vals.astype(jnp.int32))


def draw_block_table(key, part):
    return table_parts(key)[0]


def draw_lengths(key, part):
    return table_parts(key)[1]


def draw_tokens(key, part):
    key_noise = jax.random.fold_in(jax.random.fold_in(key, 13), 0)
    noise_vals = jnp.clip(jax.random.normal(key_noise, (REQUESTS, D), jnp.float32), -6.0, 6.0)
    drawn = 0.5 * noise_vals
    return drawn.astype(jnp.bfloat16)


def draw_w_query(key, part):
    drawn = jnp.clip(jax.random.normal(jax.random.fold_in(key, 11), (D, QW), jnp.float32), -6.0, 6.0) / math.sqrt(D)
    return drawn.astype(jnp.bfloat16)


def draw_k_cache(key, part):
    base_key = jax.random.fold_in(key, 12)
    key_noise = jax.random.fold_in(base_key, 0)
    cache_shape = (KV_BLOCKS, BLOCK_TOKENS, KW)
    drawn = jnp.clip(jax.random.normal(key_noise, cache_shape, jnp.float32), -6.0, 6.0)
    return drawn.astype(jnp.bfloat16)


def steps_of(stream_key, extent, shards, low, high):
    def one(dim, parts):
        steps = jax.random.uniform(jax.random.fold_in(jax.random.fold_in(stream_key, 6), dim), (parts,), jnp.float32, low / len(shards), high / len(shards))
        return jnp.repeat(jnp.exp(steps), extent[dim] // parts).reshape((-1,) + (1,) * (len(extent) - dim - 1))

    gain = one(*shards[0])
    for cut in shards[1:]:
        gain = gain * one(*cut)
    return gain


def routed_block(own_key, own, number, rows, count, top, most, slope):
    sequence = jax.random.permutation(own_key, count)
    heavy_load, ordinary = portions_of(count, rows * top, most, slope, True), portions_of(count, rows * top, most, slope, False)
    places = jnp.arange(count)

    def named(sizes, offset_by):
        used = int((sizes > 0).sum())
        fixed = max(1, used // 4)
        moved = fixed + (places - fixed + offset_by * (used - fixed)) % max(1, count - fixed)
        return jnp.zeros((count,), jnp.int32).at[sequence[jnp.where(places < fixed, places, moved)]].set(jnp.asarray(sizes, jnp.int32))

    sizes = jnp.where(number % 4 == 0, named(heavy_load, number // 4), named(ordinary, number - number // 4 - 1))
    mixed = jax.random.permutation(jax.random.fold_in(own, 3), count)
    donor, taker = mixed[0:count // 2 * 2:2], mixed[1:count // 2 * 2:2]
    slack = jnp.minimum(sizes[donor] - 1, most - sizes[taker]) // 2
    slack = jnp.where((donor == sequence[0]) | (taker == sequence[0]) | (sizes[taker] == 0), 0, jnp.maximum(slack, 0))
    moved = jax.random.randint(jax.random.fold_in(own, 4), (count // 2,), 0, 1 << 20) % (slack + 1)
    sizes = sizes.at[donor].add(-moved).at[taker].add(moved)
    labels = jnp.searchsorted(jnp.cumsum(sizes), jnp.arange(rows * top), side="right").astype(jnp.int32)
    table = labels.reshape(top, rows).T
    table = table[jax.random.permutation(jax.random.fold_in(own, 1), rows)]
    offset_by = jax.random.randint(jax.random.fold_in(own, 2), (rows, 1), 0, top)
    return jnp.take_along_axis(table, (jnp.arange(top)[None, :] + offset_by) % top, axis=1)


def portions_of(amount, total, most, slope, full):
    loads = [(1 << 20) // math.isqrt(rank ** slope) + 1 for rank in range(1, amount + 1)]
    largest = most if full else min(most, max(-(-total // amount), total * loads[0] // sum(loads)))
    least = 1 if total - largest >= amount - 1 else 0
    holding, surplus = [largest] + [least] * (amount - 1), total - largest - least * (amount - 1)
    while surplus > 0:
        movable = [i for i in range(1, amount) if holding[i] < largest] or [i for i in range(1, amount) if holding[i] < most]
        mass, remaining = sum([loads[i] for i in movable]), surplus
        for i in movable:
            extra = min(most - holding[i], max(1, remaining * loads[i] // mass), surplus)
            holding[i] = holding[i] + extra
            surplus = surplus - extra
    return np.array(holding)


def scatter_about(own_key, shape, deviation, most, shards=(), kind=jnp.bfloat16):
    values = jax.random.normal(own_key, shape, jnp.float32) * deviation
    if len(shards) > 0:
        values = steps_of(own_key, shape, shards, -0.22, 0.18) * values
    return jnp.clip(values, min=-most, max=most).astype(kind)


def setup_inputs(seed: int = 0) -> dict:
    keys = jax.random.split(jax.random.key(seed), 18)
    tokens = draw_tokens(jax.random.fold_in(keys[17], 71), 0)
    block_table = draw_block_table(jax.random.fold_in(keys[17], 71), 0)
    lengths = draw_lengths(jax.random.fold_in(keys[17], 71), 0)
    k_cache = draw_k_cache(jax.random.fold_in(keys[17], 71), 0)
    v_cache = scatter_about(keys[4], (KV_BLOCKS, BLOCK_TOKENS, KW), 1.5, 9.0, ((0, 16), (2, 2)))
    hidden_store = scatter_about(keys[5], (HIDDEN_BLOCKS, BLOCK_TOKENS, D), 1.0, 6.0, ((0, 16),))
    norm_attn = jnp.clip(1.0 + 0.1 * jax.random.normal(keys[6], (D,), jnp.float32), 0.5, 1.5).astype(jnp.bfloat16)
    w_query = draw_w_query(jax.random.fold_in(keys[17], 71), 0)
    w_key = scatter_about(keys[8], (D, KW), D ** -0.5, 0.1875, ((1, 2),))
    w_value = scatter_about(keys[9], (D, KW), D ** -0.5, 0.1875, ((1, 2),))
    w_out = scatter_about(keys[10], (QW, D), QW ** -0.5, 0.1875, ((0, 2),))
    norm_moe = jnp.clip(1.0 + 0.1 * jax.random.normal(keys[11], (D,), jnp.float32), 0.5, 1.5).astype(jnp.bfloat16)
    expert_ids_keys = jax.random.split(jax.random.fold_in(keys[12], 1), REQUESTS // REQ_DEV)
    expert_ids_turns = jax.random.permutation(jax.random.fold_in(keys[12], 3), REQUESTS // REQ_DEV)
    expert_ids = jax.vmap(lambda own, number: routed_block(jax.random.fold_in(keys[12], 2), own, number, REQ_DEV, EXPERTS, TOP, CAP, 2))(expert_ids_keys, expert_ids_turns).reshape((REQUESTS, TOP))
    gate_weights = jnp.clip(jnp.exp(math.log(1.0) - 2.3025851 * jax.random.uniform(keys[13], (REQUESTS, TOP), jnp.float32) ** steps_of(keys[13], (REQUESTS, TOP), ((0, 16),), -0.2, 0.2)), 0.1, 1.0)
    w_gate = scatter_about(keys[14], (EXPERTS, D, FF), D ** -0.5, 0.1875, ((0, 16),))
    w_up = scatter_about(keys[15], (EXPERTS, D, FF), D ** -0.5, 0.1875, ((0, 16),))
    w_down = scatter_about(keys[16], (EXPERTS, FF, D), FF ** -0.5, 0.25, ((0, 16),))
    return {"tokens": tokens, "block_table": block_table, "lengths": lengths, "k_cache": k_cache, "v_cache": v_cache, "hidden_store": hidden_store, "norm_attn": norm_attn, "w_query": w_query, "w_key": w_key, "w_value": w_value, "w_out": w_out, "norm_moe": norm_moe, "expert_ids": expert_ids, "gate_weights": gate_weights, "w_gate": w_gate, "w_up": w_up, "w_down": w_down}


NEG_FILL = -1e+30
EPSILON = 1e-05
SCORE_SCALE = 0.125

def rms_scale(row_vals, gain_row):
    mean_sq = lax.optimization_barrier(jnp.mean(row_vals * row_vals, axis=-1, keepdims=True))
    return row_vals * lax.rsqrt(mean_sq + EPSILON) * gain_row

def reference(tokens, block_table, lengths, k_cache, v_cache, hidden_store, norm_attn, w_query, w_key, w_value, w_out, norm_moe, expert_ids, gate_weights, w_gate, w_up, w_down):
    x_rows = tokens.astype(jnp.float32)
    normed = rms_scale(x_rows, norm_attn.astype(jnp.float32)).astype(jnp.bfloat16)
    queries = jnp.dot(normed, w_query, preferred_element_type=jnp.float32).astype(jnp.bfloat16)
    stored_rows = hidden_store.reshape(-1, D)
    key_new = jnp.dot(stored_rows, w_key, preferred_element_type=jnp.float32).astype(jnp.bfloat16)
    value_new = jnp.dot(stored_rows, w_value, preferred_element_type=jnp.float32).astype(jnp.bfloat16)
    every_key = jnp.concatenate([k_cache.reshape(N_POOL, NB_DEV, BLOCK_TOKENS, KW), key_new.reshape(N_POOL, NH_DEV, BLOCK_TOKENS, KW)], axis=1).reshape(TOTAL_SLOTS, BLOCK_TOKENS, KW)
    every_value = jnp.concatenate([v_cache.reshape(N_POOL, NB_DEV, BLOCK_TOKENS, KW), value_new.reshape(N_POOL, NH_DEV, BLOCK_TOKENS, KW)], axis=1).reshape(TOTAL_SLOTS, BLOCK_TOKENS, KW)
    group_width = QUERY_HEADS // KEY_VALUE_HEADS

    def one_request(packed):
        table_row, length, query_row = packed
        selected_entries = jnp.clip(table_row, 0, TOTAL_SLOTS - 1)
        key_block_list = every_key[selected_entries].reshape(REQUEST_BLOCKS, BLOCK_TOKENS, KEY_VALUE_HEADS, HEAD_SIZE).astype(jnp.float32)
        value_block_list = every_value[selected_entries].reshape(REQUEST_BLOCKS, BLOCK_TOKENS, KEY_VALUE_HEADS, HEAD_SIZE).astype(jnp.float32)
        query_head_rows = query_row.reshape(KEY_VALUE_HEADS, group_width, HEAD_SIZE).astype(jnp.float32)
        scores = jnp.einsum('gqd,btgd->bgqt', query_head_rows, key_block_list) * SCORE_SCALE
        positions = jnp.arange(REQUEST_BLOCKS)[:, None] * BLOCK_TOKENS + jnp.arange(BLOCK_TOKENS)[None, :]
        is_valid = (positions < length) & (table_row >= 0)[:, None]
        is_valid = is_valid[:, None, None, :]
        masked = jnp.where(is_valid, scores, NEG_FILL)
        block_top = lax.optimization_barrier(jnp.max(masked, axis=-1))
        weights = jnp.where(is_valid, jnp.exp(masked - block_top[..., None]), 0.0)
        block_sum = lax.optimization_barrier(jnp.sum(weights, axis=-1))
        weight_low = lax.optimization_barrier(weights.astype(jnp.bfloat16)).astype(jnp.float32)
        block_out = jnp.einsum('bgqt,btgd->bgqd', weight_low, value_block_list)
        row_top = lax.optimization_barrier(jnp.max(block_top, axis=0))
        factor = jnp.exp(block_top - row_top[None])
        total_sum = lax.optimization_barrier(jnp.sum(block_sum * factor, axis=0))
        accum = lax.optimization_barrier(jnp.sum(block_out * factor[..., None], axis=0))
        return (accum / total_sum[..., None]).reshape(QW)
    attended = lax.map(one_request, (block_table, lengths, queries)).astype(jnp.bfloat16)
    projected = jnp.dot(attended, w_out, preferred_element_type=jnp.float32)
    mixed = x_rows + projected
    normed_moe = rms_scale(mixed, norm_moe.astype(jnp.float32)).astype(jnp.bfloat16)

    def add_expert(running, expert_index):
        gate_act = jnp.dot(normed_moe, w_gate[expert_index], preferred_element_type=jnp.float32)
        up_act = jnp.dot(normed_moe, w_up[expert_index], preferred_element_type=jnp.float32)
        hidden = (jax.nn.silu(gate_act) * up_act).astype(jnp.bfloat16)
        expert_low = jnp.dot(hidden, w_down[expert_index], preferred_element_type=jnp.float32).astype(jnp.bfloat16)
        expert_out = lax.optimization_barrier(expert_low).astype(jnp.float32)
        coeff = lax.optimization_barrier(jnp.sum(jnp.where(expert_ids == expert_index, gate_weights, 0.0), axis=1))
        return (running + coeff[:, None] * expert_out, None)
    moe_out, _ = lax.scan(add_expert, jnp.zeros((REQUESTS, D), jnp.float32), jnp.arange(EXPERTS))
    return (mixed + moe_out).astype(jnp.bfloat16)
```

```python
import functools

import jax
import jax.numpy as jnp
from jax import lax
from jax.experimental import pallas as pl
from jax.experimental.pallas import tpu as pltpu
from jax.sharding import PartitionSpec as P

HEAD_SIZE = 64
LANES = 128
NEG_FILL = -1e30
EPSILON = 1e-05
SCORE_SCALE = 0.125
VMEM_LIMIT = 56 * 1024 * 1024
MESH = pl.DeviceIdType.MESH
F32 = jnp.float32
BF16 = jnp.bfloat16
VMEM = pl.BlockSpec(memory_space=pltpu.VMEM)


def rms_scale(row_vals, gain_row):
    mean_sq = jnp.mean(row_vals * row_vals, axis=-1, keepdims=True)
    return row_vals * lax.rsqrt(mean_sq + EPSILON) * gain_row


def iota(shape, dim):
    return lax.broadcasted_iota(jnp.int32, shape, dim)


def dot(a, b):
    return jnp.dot(a, b, preferred_element_type=F32)


def dot_bt(a, b):
    return lax.dot_general(a, b, (((1,), (1,)), ((), ())), preferred_element_type=F32)


def split_two(value):
    high = value.astype(BF16)
    return high, (value - high.astype(F32)).astype(BF16)


def swap_heads(row_vals, outer, inner):
    parts = []
    for i in range(inner):
        for o in range(outer):
            start = (o * inner + i) * HEAD_SIZE
            parts.append(row_vals[:, start : start + HEAD_SIZE])
    return jnp.concatenate(parts, axis=1)


def greet_pool(me, count, barrier):
    def body(k, carry):
        pl.semaphore_signal(
            barrier, inc=1, device_id={"pool": lax.rem(me + k, count)}, device_id_type=MESH
        )
        return carry

    lax.fori_loop(1, count, body, 0)


def push(src, dst, send, recv, target):
    return pltpu.make_async_remote_copy(
        src_ref=src, dst_ref=dst, send_sem=send, recv_sem=recv, device_id=target, device_id_type=MESH
    )


def gather_rows(buf, me, count, chip_send, chip_recv, core_send, core_recv):
    chips = count // 2
    chip, core = me // 2, lax.rem(me, 2)
    partner = chip * 2 + (1 - core)

    def to_chip(k):
        there = lax.rem(chip + k, chips) * 2 + core
        return push(buf.at[me], buf.at[me], chip_send.at[k], chip_recv.at[k], {"pool": there})

    def to_core(k):
        held = lax.rem(chip - k + chips, chips) * 2 + core
        return push(buf.at[held], buf.at[held], core_send.at[k], core_recv.at[k], {"pool": partner})

    def start(k, carry):
        to_chip(k).start()
        return carry

    def forward(k, carry):
        to_chip(k).wait_recv()
        to_core(k).start()
        return carry

    def finish_core(k, carry):
        to_core(k).wait()
        return carry

    def finish_chip(k, carry):
        to_chip(k).wait_send()
        return carry

    lax.fori_loop(1, chips, start, 0)
    to_core(0).start()
    lax.fori_loop(1, chips, forward, 0)
    lax.fori_loop(0, chips, finish_core, 0)
    lax.fori_loop(1, chips, finish_chip, 0)


def exchange(src, dst, me, count, send, recv):
    def copy(k):
        there = lax.rem(me + k, count)
        return push(src.at[there], dst.at[me], send.at[k], recv.at[k], {"pool": there})

    def start(k, carry):
        copy(k).start()
        return carry

    def finish(k, carry):
        copy(k).wait()
        return carry

    lax.fori_loop(1, count, start, 0)
    dst[me] = src[me]
    lax.fori_loop(1, count, finish, 0)


def query_kernel(count, groups, per_group, tok, gain, w_q, out, chip_s, chip_r, core_s, core_r):
    me = lax.axis_index("pool")
    barrier = pltpu.get_barrier_semaphore()
    greet_pool(me, count, barrier)
    normed = rms_scale(tok[...].astype(F32), gain[...].astype(F32)).astype(BF16)
    queries = swap_heads(dot(normed, w_q[...]), groups, per_group)
    out[me] = queries.astype(BF16)
    pl.semaphore_wait(barrier, count - 1)
    gather_rows(out, me, count, chip_s, chip_r, core_s, core_r)


def attend_kernel(
    steps, groups, per_group, queries, member, valid, k_blk, v_blk, hid, w_k, w_v, out,
    kn, vn, s_out, s_top, s_sum,
):
    step = pl.program_id(0)
    chunk, page, key_width = k_blk.shape
    heads = groups * per_group

    def attend(keys, values):
        rows = pl.ds(pl.multiple_of(step * chunk, chunk), chunk)
        q = dot(member[rows, :], queries[...])
        sub = iota((chunk, heads, key_width), 1)
        lane_group = iota((chunk, heads, key_width), 2) >> 6
        q_rows = jnp.zeros((chunk, heads, key_width), F32)
        for p in range(per_group):
            part = q[:, p * key_width : (p + 1) * key_width]
            q_rows = jnp.where(sub - p * groups == lane_group, part[:, None, :], q_rows)
        scores = lax.dot_general(
            q_rows.astype(BF16), keys, (((2,), (2,)), ((0,), (0,))), preferred_element_type=F32
        ) * SCORE_SCALE
        token = iota((chunk, heads, page), 2)
        is_valid = token < valid[rows, :][:, None, :]
        masked = jnp.where(is_valid, scores, NEG_FILL)
        top = jnp.max(masked, axis=-1, keepdims=True)
        weights = jnp.where(is_valid, jnp.exp(masked - top), 0.0)
        total = jnp.sum(weights, axis=-1, keepdims=True)
        mixed = lax.dot_general(
            weights.astype(BF16), values, (((2,), (1,)), ((0,), (0,))), preferred_element_type=F32
        )
        for p in range(per_group):
            piece = jnp.where(sub - p * groups == lane_group, mixed, 0.0)
            s_out[rows, p * key_width : (p + 1) * key_width] = jnp.sum(piece, axis=1)
        diag = iota((chunk, heads, LANES), 2) == iota((chunk, heads, LANES), 1)
        s_top[rows, :] = jnp.sum(jnp.where(diag, top, 0.0), axis=1)
        s_sum[rows, :] = jnp.sum(jnp.where(diag, total, 0.0), axis=1)

    @pl.when(step < steps - 1)
    def _():
        attend(k_blk[...], v_blk[...])

    @pl.when(step == steps - 1)
    def _():
        def project(n, carry):
            kn[n] = dot(hid[n], w_k[...]).astype(BF16)
            vn[n] = dot(hid[n], w_v[...]).astype(BF16)
            return carry

        lax.fori_loop(0, chunk, project, 0)
        attend(kn[...], vn[...])
        hits = member[...]
        requests = hits.shape[1]
        is_member = hits.astype(F32) > 0.5
        tops = s_top[...]
        row_id = iota((LANES, requests), 0)
        top_t = jnp.zeros((LANES, requests), F32)
        for h in range(heads):
            best = jnp.max(jnp.where(is_member, tops[:, h : h + 1], NEG_FILL), axis=0, keepdims=True)
            top_t = jnp.where(row_id == h, best, top_t)
        top_t = top_t.astype(BF16)
        factor = jnp.exp(tops - dot_bt(hits, top_t))
        eye = (iota((requests, requests), 0) == iota((requests, requests), 1)).astype(F32).astype(BF16)
        local_top = dot_bt(eye, top_t)
        width = heads * HEAD_SIZE
        spread = (iota((LANES, width), 1) >> 6 == iota((LANES, width), 0)).astype(F32).astype(BF16)
        f_high, f_low = split_two(factor)
        scaled = s_out[...] * (dot(f_high, spread) + dot(f_low, spread))

        def gather(value):
            high, low = split_two(value)
            dims = (((0,), (0,)), ((), ()))
            return lax.dot_general(hits, high, dims, preferred_element_type=F32) + lax.dot_general(
                hits, low, dims, preferred_element_type=F32
            )

        out[:, 0:width] = gather(scaled).astype(BF16)
        sum_high, sum_low = split_two(gather(s_sum[...] * factor))
        from_lane, to_lane = iota((LANES, LANES), 0), iota((LANES, LANES), 1)
        in_heads = from_lane < heads
        shift_high = (in_heads & (to_lane == from_lane + 8)).astype(F32).astype(BF16)
        shift_low = (in_heads & (to_lane == from_lane + 16)).astype(F32).astype(BF16)
        stats = local_top + dot(sum_high, shift_high) + dot(sum_low, shift_low)
        out[:, width : width + LANES] = stats.astype(BF16)


def layer_kernel(
    count, exp_count, groups, per_group,
    msg, tok, w_o, gain, ids, gates, w_g, w_u, w_d, out,
    parts, proj_out, proj_in, rows_in, mixed_buf, made, back,
    a_s, a_r, p_s, p_r, chip_s, chip_r, core_s, core_r, b_s, b_r,
):
    me = lax.axis_index("pool")
    col = lax.axis_index("exp")
    heads = groups * per_group
    width = heads * HEAD_SIZE
    barrier = pltpu.get_barrier_semaphore()
    greet_pool(me, count, barrier)
    for j in range(1, exp_count):
        pl.semaphore_signal(
            barrier, inc=1, device_id={"exp": lax.rem(col + j, exp_count)}, device_id_type=MESH
        )
    pl.semaphore_wait(barrier, count + exp_count - 2)

    exchange(msg, parts, me, count, a_s, a_r)
    rows = tok.shape[0]
    stats = parts[:, :, width : width + LANES].reshape(count * rows, LANES)
    lane, head = iota((LANES, width), 0), iota((LANES, width), 1) >> 6
    pick_top = (lane == head).astype(F32).astype(BF16)
    pick_sum = ((lane == head + 8) | (lane == head + 16)).astype(F32).astype(BF16)
    tops = dot(stats, pick_top).reshape(count, rows, width)
    sums = dot(stats, pick_sum).reshape(count, rows, width)
    best = jnp.max(tops, axis=0)
    factor = jnp.exp(tops - best[None])
    total = jnp.sum(factor * sums, axis=0)
    accum = jnp.sum(factor * parts[:, :, 0:width].astype(F32), axis=0)
    attended = swap_heads(accum / total, per_group, groups).astype(BF16)

    proj_out[...] = dot(attended, w_o[...])

    def to_exp(j):
        there = lax.rem(col + j, exp_count)
        return push(proj_out, proj_in.at[j], p_s.at[j], p_r.at[j], {"exp": there})

    for j in range(1, exp_count):
        to_exp(j).start()
    for j in range(1, exp_count):
        to_exp(j).wait()
    projected = proj_out[...]
    for j in range(1, exp_count):
        projected = projected + proj_in[j]
    mixed = tok[...].astype(F32) + projected
    mixed_buf[...] = mixed
    rows_in[me] = rms_scale(mixed, gain[...].astype(F32)).astype(BF16)
    gather_rows(rows_in, me, count, chip_s, chip_r, core_s, core_r)

    half = out.shape[1]
    cols = pl.ds(pl.multiple_of(col * half, half), half)
    everyone = rows_in[...].reshape(count * rows, tok.shape[1])
    gate_act = dot(everyone, w_g[...])
    up_act = dot(everyone, w_u[...])
    hidden = (gate_act / (1.0 + jnp.exp(-gate_act)) * up_act).astype(BF16)
    made[...] = dot(hidden, w_d[:, cols]).astype(BF16).reshape(count, rows, half)
    exchange(made, back, me, count, b_s, b_r)

    def combine(e, total):
        coeff = jnp.sum(jnp.where(ids[...] == e, gates[...], 0.0), axis=1, keepdims=True)
        return total + coeff * back[e].astype(F32)

    share = lax.fori_loop(0, count, combine, jnp.zeros((rows, half), F32))
    out[...] = (mixed_buf[:, cols] + share).astype(BF16)


def on_device(
    tokens, block_table, lengths, k_cache, v_cache, hidden_store, norm_attn, w_query, w_key, w_value,
    w_out, norm_moe, expert_ids, gate_weights, w_gate, w_up, w_down,
):
    count = lax.axis_size("pool")
    exp_count = lax.axis_size("exp")
    pool_index = lax.axis_index("pool")
    rows, model_width = tokens.shape
    width = w_query.shape[1]
    key_width = w_key.shape[1]
    groups = key_width // HEAD_SIZE
    per_group = width // key_width
    chips = count // 2
    dma = pltpu.SemaphoreType.DMA

    all_queries = pl.pallas_call(
        functools.partial(query_kernel, count, groups, per_group),
        out_shape=jax.ShapeDtypeStruct((count, rows, width), BF16),
        in_specs=[VMEM] * 3,
        out_specs=VMEM,
        scratch_shapes=[dma((chips,))] * 4,
        compiler_params=pltpu.CompilerParams(
            collective_id=0, has_side_effects=True, vmem_limit_bytes=VMEM_LIMIT
        ),
        name="queries",
    )(tokens, norm_attn.reshape(1, model_width), w_query)

    kept, page = k_cache.shape[0], k_cache.shape[1]
    chunk = hidden_store.shape[0]
    slot_count = kept + chunk
    requests, list_len = block_table.shape
    slots = pool_index * slot_count + jnp.arange(slot_count, dtype=jnp.int32)
    entry = jnp.arange(requests * list_len, dtype=jnp.int32)
    found = jnp.sum(
        jnp.where(block_table.reshape(-1)[None, :] == slots[:, None], entry[None, :], 0), axis=1
    )
    slot_req = found // list_len
    slot_block = found % list_len
    is_member = slot_req[:, None] == jnp.arange(requests, dtype=jnp.int32)[None, :]
    slot_length = jnp.sum(jnp.where(is_member, lengths[None, :], 0), axis=1)
    valid = jnp.broadcast_to((slot_length - slot_block * page)[:, None], (slot_count, page))

    steps = kept // chunk + 1
    whole = lambda shape: pl.BlockSpec(shape, lambda i: (0,) * len(shape))
    cache = pl.BlockSpec((chunk, page, key_width), lambda i: (jnp.minimum(i, steps - 2), 0, 0))
    message = pl.pallas_call(
        functools.partial(attend_kernel, steps, groups, per_group),
        grid=(steps,),
        out_shape=jax.ShapeDtypeStruct((requests, width + LANES), BF16),
        in_specs=[
            whole((requests, width)),
            whole((slot_count, requests)),
            whole((slot_count, page)),
            cache,
            cache,
            whole((chunk, page, model_width)),
            whole((model_width, key_width)),
            whole((model_width, key_width)),
        ],
        out_specs=whole((requests, width + LANES)),
        scratch_shapes=[
            pltpu.VMEM((chunk, page, key_width), BF16),
            pltpu.VMEM((chunk, page, key_width), BF16),
            pltpu.VMEM((slot_count, width), F32),
            pltpu.VMEM((slot_count, LANES), F32),
            pltpu.VMEM((slot_count, LANES), F32),
        ],
        compiler_params=pltpu.CompilerParams(
            dimension_semantics=("arbitrary",), vmem_limit_bytes=VMEM_LIMIT
        ),
        name="attend",
    )(
        all_queries.reshape(requests, width), is_member.astype(BF16), valid, k_cache, v_cache,
        hidden_store, w_key, w_value,
    )

    half = model_width // exp_count
    return pl.pallas_call(
        functools.partial(layer_kernel, count, exp_count, groups, per_group),
        out_shape=jax.ShapeDtypeStruct((rows, half), BF16),
        in_specs=[VMEM] * 9,
        out_specs=VMEM,
        scratch_shapes=[
            pltpu.VMEM((count, rows, width + LANES), BF16),
            pltpu.VMEM((rows, model_width), F32),
            pltpu.VMEM((exp_count, rows, model_width), F32),
            pltpu.VMEM((count, rows, model_width), BF16),
            pltpu.VMEM((rows, model_width), F32),
            pltpu.VMEM((count, rows, half), BF16),
            pltpu.VMEM((count, rows, half), BF16),
            dma((count,)), dma((count,)),
            dma((exp_count,)), dma((exp_count,)),
            dma((chips,)), dma((chips,)), dma((chips,)), dma((chips,)),
            dma((count,)), dma((count,)),
        ],
        compiler_params=pltpu.CompilerParams(
            collective_id=1, has_side_effects=True, vmem_limit_bytes=VMEM_LIMIT
        ),
        name="layer",
    )(
        message.reshape(count, rows, width + LANES), tokens, w_out, norm_moe.reshape(1, model_width),
        expert_ids, gate_weights, w_gate[0], w_up[0], w_down[0],
    )


def solution(mesh):
    placed = (
        P("pool", None),
        P(),
        P(),
        P("pool", None, "exp"),
        P("pool", None, "exp"),
        P("pool", None, None),
        P(),
        P(None, "exp"),
        P(None, "exp"),
        P(None, "exp"),
        P("exp", None),
        P(),
        P("pool", None),
        P("pool", None),
        P("pool", None, None),
        P("pool", None, None),
        P("pool", None, None),
    )
    return jax.shard_map(
        on_device, mesh=mesh, in_specs=placed, out_specs=P("pool", "exp"), check_vma=False
    )
```

```python
import functools

import jax
import jax.numpy as jnp
from jax import lax
from jax.experimental import pallas as pl
from jax.experimental.pallas import tpu as pltpu
from jax.sharding import PartitionSpec as P

HEAD_SIZE = 64
LANES = 128
NEG_FILL = -1e30
EPSILON = 1e-05
SCORE_SCALE = 0.125
VMEM_LIMIT = 56 * 1024 * 1024
MESH = pl.DeviceIdType.MESH
F32 = jnp.float32
BF16 = jnp.bfloat16
VMEM = pl.BlockSpec(memory_space=pltpu.VMEM)


def rms_scale(row_vals, gain_row):
    mean_sq = jnp.mean(row_vals * row_vals, axis=-1, keepdims=True)
    return row_vals * lax.rsqrt(mean_sq + EPSILON) * gain_row


def iota(shape, dim):
    return lax.broadcasted_iota(jnp.int32, shape, dim)


def dot(a, b):
    return jnp.dot(a, b, preferred_element_type=F32)


def dot_bt(a, b):
    return lax.dot_general(a, b, (((1,), (1,)), ((), ())), preferred_element_type=F32)


def split_two(value):
    high = value.astype(BF16)
    return high, (value - high.astype(F32)).astype(BF16)


def swap_heads(row_vals, outer, inner):
    parts = []
    for i in range(inner):
        for o in range(outer):
            start = (o * inner + i) * HEAD_SIZE
            parts.append(row_vals[:, start : start + HEAD_SIZE])
    return jnp.concatenate(parts, axis=1)


def greet_pool(me, count, barrier):
    def body(k, carry):
        pl.semaphore_signal(
            barrier, inc=1, device_id={"pool": lax.rem(me + k, count)}, device_id_type=MESH
        )
        return carry

    lax.fori_loop(1, count, body, 0)


def push(src, dst, send, recv, target):
    return pltpu.make_async_remote_copy(
        src_ref=src, dst_ref=dst, send_sem=send, recv_sem=recv, device_id=target, device_id_type=MESH
    )


def gather_rows(buf, me, count, chip_send, chip_recv, core_send, core_recv, early=None, late=None):
    chips = count // 2
    chip, core = me // 2, lax.rem(me, 2)
    partner = chip * 2 + (1 - core)

    def to_chip(k):
        there = lax.rem(chip + k, chips) * 2 + core
        return push(buf.at[me], buf.at[me], chip_send.at[k], chip_recv.at[k], {"pool": there})

    def to_core(k):
        held = lax.rem(chip - k + chips, chips) * 2 + core
        return push(buf.at[held], buf.at[held], core_send.at[k], core_recv.at[k], {"pool": partner})

    def start(k, carry):
        to_chip(k).start()
        return carry

    def forward(k, carry):
        to_chip(k).wait_recv()
        to_core(k).start()
        return carry

    def finish_core(k, carry):
        to_core(k).wait()
        return carry

    def finish_chip(k, carry):
        to_chip(k).wait_send()
        return carry

    lax.fori_loop(1, chips, start, 0)
    to_core(0).start()
    if early is not None:
        early()
    lax.fori_loop(1, chips, forward, 0)
    if late is not None:
        late()
    lax.fori_loop(0, chips, finish_core, 0)
    lax.fori_loop(1, chips, finish_chip, 0)


def exchange(src, dst, me, count, send, recv):
    def copy(k):
        there = lax.rem(me + k, count)
        return push(src.at[there], dst.at[me], send.at[k], recv.at[k], {"pool": there})

    def start(k, carry):
        copy(k).start()
        return carry

    def finish(k, carry):
        copy(k).wait()
        return carry

    lax.fori_loop(1, count, start, 0)
    dst[me] = src[me]
    lax.fori_loop(1, count, finish, 0)


def layer_kernel(
    count, exp_count, groups, per_group,
    tok, gain_a, gain_m, table, lengths, ids, gates, w_q_h, w_k_h, w_v_h, hid_h, k_h, v_h,
    w_o_h, w_g_h, w_u_h, w_d_h, out,
    w_q, w_k, w_v, hid, keys, values, w_o, w_g, w_u, w_d,
    queries, code, valid, s_out, s_top, s_sum,
    msg, parts, proj_out, proj_in, rows_in, mixed_buf, made, back,
    load, q_cs, q_cr, q_ps, q_pr,
    a_s, a_r, p_s, p_r, chip_s, chip_r, core_s, core_r, b_s, b_r,
):
    me = lax.axis_index("pool")
    col = lax.axis_index("exp")
    heads = groups * per_group
    width = heads * HEAD_SIZE
    rows, model_width = tok.shape
    slot_count, page, key_width = keys.shape
    kept = k_h.shape[0]
    fresh = slot_count - kept
    requests = count * rows
    barrier = pltpu.get_barrier_semaphore()
    greet_pool(me, count, barrier)
    for j in range(1, exp_count):
        pl.semaphore_signal(
            barrier, inc=1, device_id={"exp": lax.rem(col + j, exp_count)}, device_id_type=MESH
        )

    moves = [(w_q_h, w_q), (w_k_h, w_k), (w_v_h, w_v), (hid_h, hid)]
    span = kept // 4
    for n in range(4):
        part = pl.ds(n * span, span)
        moves.append((k_h.at[part], keys.at[part]))
        moves.append((v_h.at[part], values.at[part]))
    moves += [(w_o_h, w_o), (w_g_h, w_g), (w_u_h, w_u), (w_d_h, w_d)]
    loads = [pltpu.make_async_copy(s, d, load.at[n]) for n, (s, d) in enumerate(moves)]
    for item in loads:
        item.start()

    normed = rms_scale(tok[...].astype(F32), gain_a[...].astype(F32)).astype(BF16)
    loads[0].wait()
    queries[me] = swap_heads(dot(normed, w_q[...]), groups, per_group).astype(BF16)
    pl.semaphore_wait(barrier, count + exp_count - 2)

    def find_slots():
        turned = table[...].T
        place = iota(turned.shape, 0) + 1
        base = me * slot_count

        def eight(n, carry):
            for i in range(8):
                hit = jnp.where(turned == base + n * 8 + i, place, 0)
                code[pl.ds(n * 8 + i, 1), :] = jnp.sum(hit, axis=0, keepdims=True)
            return carry

        lax.fori_loop(0, slot_count // 8, eight, 0)
        found = code[...]
        left = jnp.where(found > 0, lengths[...].reshape(1, requests) - (found - 1) * page, 0)
        valid[...] = jnp.broadcast_to(jnp.sum(left, axis=1, keepdims=True), valid.shape)

    def project_hidden():
        for n in range(1, 4):
            loads[n].wait()

        def one(n, carry):
            keys[kept + n] = dot(hid[n], w_k[...]).astype(BF16)
            values[kept + n] = dot(hid[n], w_v[...]).astype(BF16)
            return carry

        lax.fori_loop(0, fresh, one, 0)

    gather_rows(queries, me, count, q_cs, q_cr, q_ps, q_pr, find_slots, project_hidden)
    for n in range(4, 12):
        loads[n].wait()

    all_queries = queries[...].reshape(requests, width)
    chunk = 48 if slot_count % 48 == 0 else 16

    def attend(step, carry):
        take = pl.ds(pl.multiple_of(step * chunk, chunk), chunk)
        q = dot((code[take, :] > 0).astype(F32).astype(BF16), all_queries)
        sub = iota((chunk, heads, key_width), 1)
        lane_group = iota((chunk, heads, key_width), 2) >> 6
        q_rows = jnp.zeros((chunk, heads, key_width), F32)
        for p in range(per_group):
            part = q[:, p * key_width : (p + 1) * key_width]
            q_rows = jnp.where(sub - p * groups == lane_group, part[:, None, :], q_rows)
        scores = lax.dot_general(
            q_rows.astype(BF16), keys[take], (((2,), (2,)), ((0,), (0,))), preferred_element_type=F32
        ) * SCORE_SCALE
        token = iota((chunk, heads, page), 2)
        is_valid = token < valid[take, :][:, None, :]
        masked = jnp.where(is_valid, scores, NEG_FILL)
        top = jnp.max(masked, axis=-1, keepdims=True)
        weights = jnp.where(is_valid, jnp.exp(masked - top), 0.0)
        total = jnp.sum(weights, axis=-1, keepdims=True)
        mixed = lax.dot_general(
            weights.astype(BF16), values[take], (((2,), (1,)), ((0,), (0,))),
            preferred_element_type=F32,
        )
        for p in range(per_group):
            piece = jnp.where(sub - p * groups == lane_group, mixed, 0.0)
            s_out[take, p * key_width : (p + 1) * key_width] = jnp.sum(piece, axis=1)
        diag = iota((chunk, heads, LANES), 2) == iota((chunk, heads, LANES), 1)
        s_top[take, :] = jnp.sum(jnp.where(diag, top, 0.0), axis=1)
        s_sum[take, :] = jnp.sum(jnp.where(diag, total, 0.0), axis=1)
        return carry

    lax.fori_loop(0, slot_count // chunk, attend, 0)

    is_member = code[...] > 0
    hits = is_member.astype(F32).astype(BF16)
    tops = s_top[...]
    row_id = iota((LANES, requests), 0)
    top_t = jnp.zeros((LANES, requests), F32)
    for h in range(heads):
        best = jnp.max(jnp.where(is_member, tops[:, h : h + 1], NEG_FILL), axis=0, keepdims=True)
        top_t = jnp.where(row_id == h, best, top_t)
    top_t = top_t.astype(BF16)
    factor = jnp.exp(tops - dot_bt(hits, top_t))
    eye = (iota((requests, requests), 0) == iota((requests, requests), 1)).astype(F32).astype(BF16)
    local_top = dot_bt(eye, top_t)
    spread = (iota((LANES, width), 1) >> 6 == iota((LANES, width), 0)).astype(F32).astype(BF16)
    f_high, f_low = split_two(factor)
    scaled = s_out[...] * (dot(f_high, spread) + dot(f_low, spread))

    def by_request(value):
        high, low = split_two(value)
        dims = (((0,), (0,)), ((), ()))
        return lax.dot_general(hits, high, dims, preferred_element_type=F32) + lax.dot_general(
            hits, low, dims, preferred_element_type=F32
        )

    msg[:, :, 0:width] = by_request(scaled).astype(BF16).reshape(count, rows, width)
    sum_high, sum_low = split_two(by_request(s_sum[...] * factor))
    from_lane, to_lane = iota((LANES, LANES), 0), iota((LANES, LANES), 1)
    in_heads = from_lane < heads
    shift_high = (in_heads & (to_lane == from_lane + 8)).astype(F32).astype(BF16)
    shift_low = (in_heads & (to_lane == from_lane + 16)).astype(F32).astype(BF16)
    stats = local_top + dot(sum_high, shift_high) + dot(sum_low, shift_low)
    msg[:, :, width : width + LANES] = stats.astype(BF16).reshape(count, rows, LANES)

    exchange(msg, parts, me, count, a_s, a_r)
    stats = parts[:, :, width : width + LANES].reshape(count * rows, LANES)
    lane, head = iota((LANES, width), 0), iota((LANES, width), 1) >> 6
    pick_top = (lane == head).astype(F32).astype(BF16)
    pick_sum = ((lane == head + 8) | (lane == head + 16)).astype(F32).astype(BF16)
    tops = dot(stats, pick_top).reshape(count, rows, width)
    sums = dot(stats, pick_sum).reshape(count, rows, width)
    best = jnp.max(tops, axis=0)
    factor = jnp.exp(tops - best[None])
    total = jnp.sum(factor * sums, axis=0)
    accum = jnp.sum(factor * parts[:, :, 0:width].astype(F32), axis=0)
    attended = swap_heads(accum / total, per_group, groups).astype(BF16)

    for n in range(12, 16):
        loads[n].wait()
    proj_out[...] = dot(attended, w_o[...])

    def to_exp(j):
        there = lax.rem(col + j, exp_count)
        return push(proj_out, proj_in.at[j], p_s.at[j], p_r.at[j], {"exp": there})

    for j in range(1, exp_count):
        to_exp(j).start()
    for j in range(1, exp_count):
        to_exp(j).wait()
    projected = proj_out[...]
    for j in range(1, exp_count):
        projected = projected + proj_in[j]
    mixed = tok[...].astype(F32) + projected
    mixed_buf[...] = mixed
    rows_in[me] = rms_scale(mixed, gain_m[...].astype(F32)).astype(BF16)
    gather_rows(rows_in, me, count, chip_s, chip_r, core_s, core_r)

    half = out.shape[1]
    cols = pl.ds(pl.multiple_of(col * half, half), half)
    everyone = rows_in[...].reshape(count * rows, tok.shape[1])
    gate_act = dot(everyone, w_g[...])
    up_act = dot(everyone, w_u[...])
    hidden = (gate_act / (1.0 + jnp.exp(-gate_act)) * up_act).astype(BF16)
    made[...] = dot(hidden, w_d[:, cols]).astype(BF16).reshape(count, rows, half)
    exchange(made, back, me, count, b_s, b_r)

    def combine(e, total):
        coeff = jnp.sum(jnp.where(ids[...] == e, gates[...], 0.0), axis=1, keepdims=True)
        return total + coeff * back[e].astype(F32)

    share = lax.fori_loop(0, count, combine, jnp.zeros((rows, half), F32))
    out[...] = (mixed_buf[:, cols] + share).astype(BF16)


def on_device(
    tokens, block_table, lengths, k_cache, v_cache, hidden_store, norm_attn, w_query, w_key, w_value,
    w_out, norm_moe, expert_ids, gate_weights, w_gate, w_up, w_down,
):
    count = lax.axis_size("pool")
    exp_count = lax.axis_size("exp")
    rows, model_width = tokens.shape
    width = w_query.shape[1]
    key_width = w_key.shape[1]
    groups = key_width // HEAD_SIZE
    per_group = width // key_width
    chips = count // 2
    dma = pltpu.SemaphoreType.DMA
    page = k_cache.shape[1]
    slot_count = k_cache.shape[0] + hidden_store.shape[0]
    requests = block_table.shape[0]
    half = model_width // exp_count
    hidden_units = w_gate.shape[2]
    big = pl.BlockSpec(memory_space=pl.ANY)
    return pl.pallas_call(
        functools.partial(layer_kernel, count, exp_count, groups, per_group),
        out_shape=jax.ShapeDtypeStruct((rows, half), BF16),
        in_specs=[VMEM] * 7 + [big] * 10,
        out_specs=VMEM,
        scratch_shapes=[
            pltpu.VMEM(w_query.shape, BF16),
            pltpu.VMEM(w_key.shape, BF16),
            pltpu.VMEM(w_value.shape, BF16),
            pltpu.VMEM(hidden_store.shape, BF16),
            pltpu.VMEM((slot_count, page, key_width), BF16),
            pltpu.VMEM((slot_count, page, key_width), BF16),
            pltpu.VMEM(w_out.shape, BF16),
            pltpu.VMEM((model_width, hidden_units), BF16),
            pltpu.VMEM((model_width, hidden_units), BF16),
            pltpu.VMEM((hidden_units, model_width), BF16),
            pltpu.VMEM((count, rows, width), BF16),
            pltpu.VMEM((slot_count, requests), jnp.int32),
            pltpu.VMEM((slot_count, page), jnp.int32),
            pltpu.VMEM((slot_count, width), F32),
            pltpu.VMEM((slot_count, LANES), F32),
            pltpu.VMEM((slot_count, LANES), F32),
            pltpu.VMEM((count, rows, width + LANES), BF16),
            pltpu.VMEM((count, rows, width + LANES), BF16),
            pltpu.VMEM((rows, model_width), F32),
            pltpu.VMEM((exp_count, rows, model_width), F32),
            pltpu.VMEM((count, rows, model_width), BF16),
            pltpu.VMEM((rows, model_width), F32),
            pltpu.VMEM((count, rows, half), BF16),
            pltpu.VMEM((count, rows, half), BF16),
            dma((16,)),
            dma((chips,)), dma((chips,)), dma((chips,)), dma((chips,)),
            dma((count,)), dma((count,)),
            dma((exp_count,)), dma((exp_count,)),
            dma((chips,)), dma((chips,)), dma((chips,)), dma((chips,)),
            dma((count,)), dma((count,)),
        ],
        compiler_params=pltpu.CompilerParams(
            collective_id=0, has_side_effects=True, vmem_limit_bytes=VMEM_LIMIT
        ),
        name="layer",
    )(
        tokens, norm_attn.reshape(1, -1), norm_moe.reshape(1, -1), block_table, lengths,
        expert_ids, gate_weights, w_query, w_key, w_value, hidden_store, k_cache, v_cache,
        w_out, w_gate[0], w_up[0], w_down[0],
    )


def solution(mesh):
    placed = (
        P("pool", None),
        P(),
        P(),
        P("pool", None, "exp"),
        P("pool", None, "exp"),
        P("pool", None, None),
        P(),
        P(None, "exp"),
        P(None, "exp"),
        P(None, "exp"),
        P("exp", None),
        P(),
        P("pool", None),
        P("pool", None),
        P("pool", None, None),
        P("pool", None, None),
        P("pool", None, None),
    )
    return jax.shard_map(
        on_device, mesh=mesh, in_specs=placed, out_specs=P("pool", "exp"), check_vma=False
    )
```

```python
import functools

import jax
import jax.numpy as jnp
from jax import lax
from jax.experimental import pallas as pl
from jax.experimental.pallas import tpu as pltpu
from jax.sharding import PartitionSpec as P

HEAD_SIZE = 64
LANES = 128
NEG_FILL = -1e30
EPSILON = 1e-05
SCORE_SCALE = 0.125
VMEM_LIMIT = 56 * 1024 * 1024
MESH = pl.DeviceIdType.MESH
F32 = jnp.float32
BF16 = jnp.bfloat16
VMEM = pl.BlockSpec(memory_space=pltpu.VMEM)


def rms_scale(row_vals, gain_row):
    mean_sq = jnp.mean(row_vals * row_vals, axis=-1, keepdims=True)
    return row_vals * lax.rsqrt(mean_sq + EPSILON) * gain_row


def iota(shape, dim):
    return lax.broadcasted_iota(jnp.int32, shape, dim)


def dot(a, b):
    return jnp.dot(a, b, preferred_element_type=F32)


def dot_bt(a, b):
    return lax.dot_general(a, b, (((1,), (1,)), ((), ())), preferred_element_type=F32)


def split_two(value):
    high = value.astype(BF16)
    return high, (value - high.astype(F32)).astype(BF16)


def swap_heads(row_vals, outer, inner):
    parts = []
    for i in range(inner):
        for o in range(outer):
            start = (o * inner + i) * HEAD_SIZE
            parts.append(row_vals[:, start : start + HEAD_SIZE])
    return jnp.concatenate(parts, axis=1)


def greet_pool(me, count, barrier):
    def body(k, carry):
        pl.semaphore_signal(
            barrier, inc=1, device_id={"pool": lax.rem(me + k, count)}, device_id_type=MESH
        )
        return carry

    lax.fori_loop(1, count, body, 0)


def push(src, dst, send, recv, target):
    return pltpu.make_async_remote_copy(
        src_ref=src, dst_ref=dst, send_sem=send, recv_sem=recv, device_id=target, device_id_type=MESH
    )


def gather_rows(buf, me, count, chip_send, chip_recv, core_send, core_recv, early=None, late=None):
    chips = count // 2
    chip, core = me // 2, lax.rem(me, 2)
    partner = chip * 2 + (1 - core)

    def to_chip(k):
        there = lax.rem(chip + k, chips) * 2 + core
        return push(buf.at[me], buf.at[me], chip_send.at[k], chip_recv.at[k], {"pool": there})

    def to_core(k):
        held = lax.rem(chip - k + chips, chips) * 2 + core
        return push(buf.at[held], buf.at[held], core_send.at[k], core_recv.at[k], {"pool": partner})

    def start(k, carry):
        to_chip(k).start()
        return carry

    def forward(k, carry):
        to_chip(k).wait_recv()
        to_core(k).start()
        return carry

    def finish_core(k, carry):
        to_core(k).wait()
        return carry

    def finish_chip(k, carry):
        to_chip(k).wait_send()
        return carry

    lax.fori_loop(1, chips, start, 0)
    to_core(0).start()
    if early is not None:
        early()
    lax.fori_loop(1, chips, forward, 0)
    if late is not None:
        late()
    lax.fori_loop(0, chips, finish_core, 0)
    lax.fori_loop(1, chips, finish_chip, 0)


def exchange(src, dst, me, count, send, recv):
    def copy(k):
        there = lax.rem(me + k, count)
        return push(src.at[there], dst.at[me], send.at[k], recv.at[k], {"pool": there})

    def start(k, carry):
        copy(k).start()
        return carry

    def finish(k, carry):
        copy(k).wait()
        return carry

    lax.fori_loop(1, count, start, 0)
    dst[me] = src[me]
    lax.fori_loop(1, count, finish, 0)


def layer_kernel(
    count, exp_count, groups, per_group,
    tok, gain_a, gain_m, table, lengths, ids, gates, w_q_h, w_k_h, w_v_h, hid_h, k_h, v_h,
    w_o_h, w_g_h, w_u_h, w_d_h, out,
    w_q, w_k, w_v, hid, keys, values, w_o, w_g, w_u, w_d,
    queries, code, valid, s_out, s_top, s_sum,
    msg, parts, proj_out, proj_in, rows_in, mixed_buf, made, back, coeff,
    load, q_cs, q_cr, q_ps, q_pr,
    a_s, a_r, p_s, p_r, chip_s, chip_r, core_s, core_r, b_s, b_r,
):
    me = lax.axis_index("pool")
    col = lax.axis_index("exp")
    heads = groups * per_group
    width = heads * HEAD_SIZE
    rows, model_width = tok.shape
    slot_count, page, key_width = keys.shape
    kept = k_h.shape[0]
    fresh = slot_count - kept
    requests = count * rows
    barrier = pltpu.get_barrier_semaphore()
    greet_pool(me, count, barrier)
    for j in range(1, exp_count):
        pl.semaphore_signal(
            barrier, inc=1, device_id={"exp": lax.rem(col + j, exp_count)}, device_id_type=MESH
        )

    moves = [(w_q_h, w_q), (w_k_h, w_k), (w_v_h, w_v), (hid_h, hid)]
    span = kept // 4
    for n in range(4):
        part = pl.ds(n * span, span)
        moves.append((k_h.at[part], keys.at[part]))
        moves.append((v_h.at[part], values.at[part]))
    moves += [(w_o_h, w_o), (w_g_h, w_g), (w_u_h, w_u), (w_d_h, w_d)]
    loads = [pltpu.make_async_copy(s, d, load.at[n]) for n, (s, d) in enumerate(moves)]
    loads[0].start()

    normed = rms_scale(tok[...].astype(F32), gain_a[...].astype(F32).reshape(1, model_width)).astype(BF16)
    loads[0].wait()
    for item in loads[1:]:
        item.start()
    queries[me] = swap_heads(dot(normed, w_q[...]), groups, per_group).astype(BF16)
    pl.semaphore_wait(barrier, count + exp_count - 2)

    def find_slots():
        turned = table[...].T
        place = iota(turned.shape, 0) + 1
        base = me * slot_count

        def eight(n, carry):
            for i in range(8):
                hit = jnp.where(turned == base + n * 8 + i, place, 0)
                code[pl.ds(n * 8 + i, 1), :] = jnp.sum(hit, axis=0, keepdims=True)
            return carry

        lax.fori_loop(0, slot_count // 8, eight, 0)
        found = code[...]
        left = jnp.where(found > 0, lengths[...].reshape(1, requests) - (found - 1) * page, 0)
        valid[...] = jnp.broadcast_to(jnp.sum(left, axis=1, keepdims=True), valid.shape)

    def project_hidden():
        for n in range(1, 4):
            loads[n].wait()

        def one(n, carry):
            keys[kept + n] = dot(hid[n], w_k[...]).astype(BF16)
            values[kept + n] = dot(hid[n], w_v[...]).astype(BF16)
            return carry

        lax.fori_loop(0, fresh, one, 0)

    gather_rows(queries, me, count, q_cs, q_cr, q_ps, q_pr, find_slots, project_hidden)
    for n in range(4, 12):
        loads[n].wait()

    all_queries = queries[...].reshape(requests, width)
    chunk = 48 if slot_count % 48 == 0 else 16

    def attend(step, carry):
        take = pl.ds(pl.multiple_of(step * chunk, chunk), chunk)
        q = dot((code[take, :] > 0).astype(F32).astype(BF16), all_queries)
        sub = iota((chunk, heads, key_width), 1)
        lane_group = iota((chunk, heads, key_width), 2) >> 6
        q_rows = jnp.zeros((chunk, heads, key_width), F32)
        for p in range(per_group):
            part = q[:, p * key_width : (p + 1) * key_width]
            q_rows = jnp.where(sub - p * groups == lane_group, part[:, None, :], q_rows)
        scores = lax.dot_general(
            q_rows.astype(BF16), keys[take], (((2,), (2,)), ((0,), (0,))), preferred_element_type=F32
        ) * SCORE_SCALE
        token = iota((chunk, heads, page), 2)
        is_valid = token < valid[take, :][:, None, :]
        masked = jnp.where(is_valid, scores, NEG_FILL)
        top = jnp.max(masked, axis=-1, keepdims=True)
        weights = jnp.where(is_valid, jnp.exp(masked - top), 0.0)
        total = jnp.sum(weights, axis=-1, keepdims=True)
        mixed = lax.dot_general(
            weights.astype(BF16), values[take], (((2,), (1,)), ((0,), (0,))),
            preferred_element_type=F32,
        )
        for p in range(per_group):
            piece = jnp.where(sub - p * groups == lane_group, mixed, 0.0)
            s_out[take, p * key_width : (p + 1) * key_width] = jnp.sum(piece, axis=1)
        diag = iota((chunk, heads, LANES), 2) == iota((chunk, heads, LANES), 1)
        s_top[take, :] = jnp.sum(jnp.where(diag, top, 0.0), axis=1)
        s_sum[take, :] = jnp.sum(jnp.where(diag, total, 0.0), axis=1)
        return carry

    lax.fori_loop(0, slot_count // chunk, attend, 0)

    is_member = code[...] > 0
    hits = is_member.astype(F32).astype(BF16)
    tops = s_top[...]
    row_id = iota((LANES, requests), 0)
    top_t = jnp.zeros((LANES, requests), F32)
    for h in range(heads):
        best = jnp.max(jnp.where(is_member, tops[:, h : h + 1], NEG_FILL), axis=0, keepdims=True)
        top_t = jnp.where(row_id == h, best, top_t)
    top_t = top_t.astype(BF16)
    factor = jnp.exp(tops - dot_bt(hits, top_t))
    eye = (iota((requests, requests), 0) == iota((requests, requests), 1)).astype(F32).astype(BF16)
    local_top = dot_bt(eye, top_t)
    spread = (iota((LANES, width), 1) >> 6 == iota((LANES, width), 0)).astype(F32).astype(BF16)
    f_high, f_low = split_two(factor)
    scaled = s_out[...] * (dot(f_high, spread) + dot(f_low, spread))

    def by_request(value):
        high, low = split_two(value)
        dims = (((0,), (0,)), ((), ()))
        return lax.dot_general(hits, high, dims, preferred_element_type=F32) + lax.dot_general(
            hits, low, dims, preferred_element_type=F32
        )

    msg[:, :, 0:width] = by_request(scaled).astype(BF16).reshape(count, rows, width)
    sum_high, sum_low = split_two(by_request(s_sum[...] * factor))
    from_lane, to_lane = iota((LANES, LANES), 0), iota((LANES, LANES), 1)
    in_heads = from_lane < heads
    shift_high = (in_heads & (to_lane == from_lane + 8)).astype(F32).astype(BF16)
    shift_low = (in_heads & (to_lane == from_lane + 16)).astype(F32).astype(BF16)
    stats = local_top + dot(sum_high, shift_high) + dot(sum_low, shift_low)
    msg[:, :, width : width + LANES] = stats.astype(BF16).reshape(count, rows, LANES)

    exchange(msg, parts, me, count, a_s, a_r)
    stats = parts[:, :, width : width + LANES].reshape(count * rows, LANES)
    lane, head = iota((LANES, width), 0), iota((LANES, width), 1) >> 6
    pick_top = (lane == head).astype(F32).astype(BF16)
    pick_sum = ((lane == head + 8) | (lane == head + 16)).astype(F32).astype(BF16)
    tops = dot(stats, pick_top).reshape(count, rows, width)
    sums = dot(stats, pick_sum).reshape(count, rows, width)
    best = jnp.max(tops, axis=0)
    factor = jnp.exp(tops - best[None])
    total = jnp.sum(factor * sums, axis=0)
    accum = jnp.sum(factor * parts[:, :, 0:width].astype(F32), axis=0)
    attended = swap_heads(accum / total, per_group, groups).astype(BF16)

    for n in range(12, 16):
        loads[n].wait()
    proj_out[...] = dot(attended, w_o[...]).astype(BF16)

    def to_exp(j):
        there = lax.rem(col + j, exp_count)
        return push(proj_out, proj_in.at[j], p_s.at[j], p_r.at[j], {"exp": there})

    for j in range(1, exp_count):
        to_exp(j).start()
    for j in range(1, exp_count):
        to_exp(j).wait()
    projected = proj_out[...].astype(F32)
    for j in range(1, exp_count):
        projected = projected + proj_in[j].astype(F32)
    mixed = tok[...].astype(F32) + projected
    mixed_buf[...] = mixed
    chips = count // 2
    chip, core = me // 2, lax.rem(me, 2)
    partner = chip * 2 + (1 - core)
    rows_in[core] = rms_scale(
        mixed, gain_m[...].astype(F32).reshape(1, model_width)
    ).astype(BF16)

    def to_chip(k):
        there = lax.rem(chip + k, chips) * 2 + core
        return push(
            rows_in.at[core], rows_in.at[k * 2 + core], chip_s.at[k], chip_r.at[k], {"pool": there}
        )

    def to_core(k):
        held = rows_in.at[k * 2 + core]
        return push(held, held, core_s.at[k], core_r.at[k], {"pool": partner})

    def start_chip(k, carry):
        to_chip(k).start()
        return carry

    lax.fori_loop(1, chips, start_chip, 0)
    to_core(0).start()

    half = out.shape[1]
    cols = pl.ds(pl.multiple_of(col * half, half), half)

    def give(i):
        k, there_core = i // 2, lax.rem(i, 2)
        there = lax.rem(chip - k + chips, chips) * 2 + there_core
        return push(
            made.at[i], back.at[me], b_s.at[i], b_r.at[k * 2 + core], {"pool": there}
        )

    def forward(k, carry):
        to_chip(k).wait_recv()
        to_core(k).start()
        return carry

    def finish_core(k, carry):
        to_core(k).wait_recv()
        return carry

    def start_give(i, carry):
        give(i).start()
        return carry

    near = chips // 2
    for low, high in ((0, near), (near, chips)):
        lax.fori_loop(max(low, 1), high, forward, 0)
        lax.fori_loop(low, high, finish_core, 0)
        some = rows_in[2 * low : 2 * high].reshape((high - low) * 2 * rows, model_width)
        gate_act = dot(some, w_g[...])
        up_act = dot(some, w_u[...])
        hidden = (gate_act / (1.0 + jnp.exp(-gate_act)) * up_act).astype(BF16)
        result = dot(hidden, w_d[:, cols]).astype(BF16)
        made[2 * low : 2 * high] = result.reshape((high - low) * 2, rows, half)
        if low == 0:
            give(1 - core).start()
        lax.fori_loop(2 * max(low, 1), 2 * high, start_give, 0)

    eye_rows = iota((rows, rows), 0) == iota((rows, rows), 1)

    def weigh(e, carry):
        line = jnp.sum(jnp.where(ids[...] == e, gates[...], 0.0), axis=0, keepdims=True)
        column = jnp.sum(jnp.where(eye_rows, line, 0.0), axis=1, keepdims=True)
        coeff[e] = jnp.broadcast_to(column, (rows, LANES))
        return carry

    lax.fori_loop(0, count, weigh, 0)

    def arrival(j):
        k, from_core = j // 2, lax.rem(j, 2)
        source = lax.rem(chip + k, chips) * 2 + from_core
        return source, push(
            made.at[0], back.at[source], b_s.at[j], b_r.at[j], {"pool": partner}
        )

    own = made[core].astype(F32) * coeff[me][:, 0:1]
    total = mixed_buf[:, cols] + own
    _, first = arrival(1 - core)
    first.wait_recv()
    total = total + coeff[partner][:, 0:1] * back[partner].astype(F32)

    def combine(j, total):
        source, copy = arrival(j)
        copy.wait_recv()
        return total + coeff[source][:, 0:1] * back[source].astype(F32)

    out[...] = lax.fori_loop(2, count, combine, total).astype(BF16)

    def drain_give(i, carry):
        give(i).wait_send()
        return carry

    def drain_chip(k, carry):
        to_chip(k).wait_send()
        return carry

    def drain_core(k, carry):
        to_core(k).wait_send()
        return carry

    give(1 - core).wait_send()
    lax.fori_loop(2, count, drain_give, 0)
    lax.fori_loop(1, chips, drain_chip, 0)
    lax.fori_loop(0, chips, drain_core, 0)


def on_device(
    tokens, block_table, lengths, k_cache, v_cache, hidden_store, norm_attn, w_query, w_key, w_value,
    w_out, norm_moe, expert_ids, gate_weights, w_gate, w_up, w_down,
):
    count = lax.axis_size("pool")
    exp_count = lax.axis_size("exp")
    rows, model_width = tokens.shape
    width = w_query.shape[1]
    key_width = w_key.shape[1]
    groups = key_width // HEAD_SIZE
    per_group = width // key_width
    chips = count // 2
    dma = pltpu.SemaphoreType.DMA
    page = k_cache.shape[1]
    slot_count = k_cache.shape[0] + hidden_store.shape[0]
    requests = block_table.shape[0]
    half = model_width // exp_count
    hidden_units = w_gate.shape[2]
    big = pl.BlockSpec(memory_space=pl.ANY)
    return pl.pallas_call(
        functools.partial(layer_kernel, count, exp_count, groups, per_group),
        out_shape=jax.ShapeDtypeStruct((rows, half), BF16),
        in_specs=[VMEM] * 7 + [big] * 10,
        out_specs=VMEM,
        scratch_shapes=[
            pltpu.VMEM(w_query.shape, BF16),
            pltpu.VMEM(w_key.shape, BF16),
            pltpu.VMEM(w_value.shape, BF16),
            pltpu.VMEM(hidden_store.shape, BF16),
            pltpu.VMEM((slot_count, page, key_width), BF16),
            pltpu.VMEM((slot_count, page, key_width), BF16),
            pltpu.VMEM(w_out.shape, BF16),
            pltpu.VMEM((model_width, hidden_units), BF16),
            pltpu.VMEM((model_width, hidden_units), BF16),
            pltpu.VMEM((hidden_units, model_width), BF16),
            pltpu.VMEM((count, rows, width), BF16),
            pltpu.VMEM((slot_count, requests), jnp.int32),
            pltpu.VMEM((slot_count, page), jnp.int32),
            pltpu.VMEM((slot_count, width), F32),
            pltpu.VMEM((slot_count, LANES), F32),
            pltpu.VMEM((slot_count, LANES), F32),
            pltpu.VMEM((count, rows, width + LANES), BF16),
            pltpu.VMEM((count, rows, width + LANES), BF16),
            pltpu.VMEM((rows, model_width), BF16),
            pltpu.VMEM((exp_count, rows, model_width), BF16),
            pltpu.VMEM((count, rows, model_width), BF16),
            pltpu.VMEM((rows, model_width), F32),
            pltpu.VMEM((count, rows, half), BF16),
            pltpu.VMEM((count, rows, half), BF16),
            pltpu.VMEM((count, rows, LANES), F32),
            dma((16,)),
            dma((chips,)), dma((chips,)), dma((chips,)), dma((chips,)),
            dma((count,)), dma((count,)),
            dma((exp_count,)), dma((exp_count,)),
            dma((chips,)), dma((chips,)), dma((chips,)), dma((chips,)),
            dma((count,)), dma((count,)),
        ],
        compiler_params=pltpu.CompilerParams(
            collective_id=0, has_side_effects=True, vmem_limit_bytes=VMEM_LIMIT
        ),
        name="layer",
    )(
        tokens, norm_attn, norm_moe, block_table, lengths,
        expert_ids.T, gate_weights.T, w_query, w_key, w_value, hidden_store, k_cache, v_cache,
        w_out, w_gate[0], w_up[0], w_down[0],
    )


def solution(mesh):
    placed = (
        P("pool", None),
        P(),
        P(),
        P("pool", None, "exp"),
        P("pool", None, "exp"),
        P("pool", None, None),
        P(),
        P(None, "exp"),
        P(None, "exp"),
        P(None, "exp"),
        P("exp", None),
        P(),
        P("pool", None),
        P("pool", None),
        P("pool", None, None),
        P("pool", None, None),
        P("pool", None, None),
    )
    return jax.shard_map(
        on_device, mesh=mesh, in_specs=placed, out_specs=P("pool", "exp"), check_vma=False
    )
```

```python
import functools

import jax
import jax.numpy as jnp
from jax import lax
from jax.experimental import pallas as pl
from jax.experimental.pallas import tpu as pltpu
from jax.sharding import PartitionSpec as P

HEAD_SIZE = 64
LANES = 128
NEG_FILL = -1e30
EPSILON = 1e-05
SCORE_SCALE = 0.125
VMEM_LIMIT = 56 * 1024 * 1024
MESH = pl.DeviceIdType.MESH
F32 = jnp.float32
BF16 = jnp.bfloat16
VMEM = pl.BlockSpec(memory_space=pltpu.VMEM)


def rms_scale(row_vals, gain_row):
    mean_sq = jnp.mean(row_vals * row_vals, axis=-1, keepdims=True)
    return row_vals * lax.rsqrt(mean_sq + EPSILON) * gain_row


def iota(shape, dim):
    return lax.broadcasted_iota(jnp.int32, shape, dim)


def dot(a, b):
    return jnp.dot(a, b, preferred_element_type=F32)


def dot_bt(a, b):
    return lax.dot_general(a, b, (((1,), (1,)), ((), ())), preferred_element_type=F32)


def split_two(value):
    high = value.astype(BF16)
    return high, (value - high.astype(F32)).astype(BF16)


def swap_heads(row_vals, outer, inner):
    parts = []
    for i in range(inner):
        for o in range(outer):
            start = (o * inner + i) * HEAD_SIZE
            parts.append(row_vals[:, start : start + HEAD_SIZE])
    return jnp.concatenate(parts, axis=1)


def greet_pool(me, count, barrier):
    def body(k, carry):
        pl.semaphore_signal(
            barrier, inc=1, device_id={"pool": lax.rem(me + k, count)}, device_id_type=MESH
        )
        return carry

    lax.fori_loop(1, count, body, 0)


def push(src, dst, send, recv, target):
    return pltpu.make_async_remote_copy(
        src_ref=src, dst_ref=dst, send_sem=send, recv_sem=recv, device_id=target, device_id_type=MESH
    )


def gather_rows(buf, me, count, chip_send, chip_recv, core_send, core_recv, early=None, late=None):
    chips = count // 2
    chip, core = me // 2, lax.rem(me, 2)
    partner = chip * 2 + (1 - core)

    def to_chip(k):
        there = lax.rem(chip + k, chips) * 2 + core
        return push(buf.at[me], buf.at[me], chip_send.at[k], chip_recv.at[k], {"pool": there})

    def to_core(k):
        held = lax.rem(chip - k + chips, chips) * 2 + core
        return push(buf.at[held], buf.at[held], core_send.at[k], core_recv.at[k], {"pool": partner})

    def start(k, carry):
        to_chip(k).start()
        return carry

    def forward(k, carry):
        to_chip(k).wait_recv()
        to_core(k).start()
        return carry

    def finish_core(k, carry):
        to_core(k).wait()
        return carry

    def finish_chip(k, carry):
        to_chip(k).wait_send()
        return carry

    lax.fori_loop(1, chips, start, 0)
    to_core(0).start()
    if early is not None:
        early()
    lax.fori_loop(1, chips, forward, 0)
    if late is not None:
        late()
    lax.fori_loop(0, chips, finish_core, 0)
    lax.fori_loop(1, chips, finish_chip, 0)


def exchange(src, dst, me, count, send, recv):
    def copy(k):
        there = lax.rem(me + k, count)
        return push(src.at[there], dst.at[me], send.at[k], recv.at[k], {"pool": there})

    def start(k, carry):
        copy(k).start()
        return carry

    def finish(k, carry):
        copy(k).wait()
        return carry

    lax.fori_loop(1, count, start, 0)
    dst[me] = src[me]
    lax.fori_loop(1, count, finish, 0)


def layer_kernel(
    count, exp_count, groups, per_group,
    tok, gain_a, gain_m, table, lengths, ids, gates, w_q_h, w_k_h, w_v_h, hid_h, k_h, v_h,
    w_o_h, w_g_h, w_u_h, w_d_h, out,
    w_q, w_k, w_v, hid, keys, values, w_o, w_g, w_u, w_d,
    queries, code, valid, s_out, s_top, s_sum,
    msg, parts, proj_out, proj_in, rows_in, mixed_buf, made, back, coeff,
    load, q_cs, q_cr, q_ps, q_pr,
    a_s, a_r, p_s, p_r, chip_s, chip_r, core_s, core_r, b_s, b_r,
):
    me = lax.axis_index("pool")
    col = lax.axis_index("exp")
    heads = groups * per_group
    width = heads * HEAD_SIZE
    rows, model_width = tok.shape
    slot_count, page, key_width = keys.shape
    kept = k_h.shape[0]
    fresh = slot_count - kept
    requests = count * rows
    barrier = pltpu.get_barrier_semaphore()
    greet_pool(me, count, barrier)
    for j in range(1, exp_count):
        pl.semaphore_signal(
            barrier, inc=1, device_id={"exp": lax.rem(col + j, exp_count)}, device_id_type=MESH
        )

    moves = [(w_q_h, w_q), (w_k_h, w_k), (w_v_h, w_v), (hid_h, hid)]
    span = kept // 4
    for n in range(4):
        part = pl.ds(n * span, span)
        moves.append((k_h.at[part], keys.at[part]))
        moves.append((v_h.at[part], values.at[part]))
    moves += [(w_o_h, w_o), (w_g_h, w_g), (w_u_h, w_u), (w_d_h, w_d)]
    loads = [pltpu.make_async_copy(s, d, load.at[n]) for n, (s, d) in enumerate(moves)]
    loads[0].start()

    normed = rms_scale(tok[...].astype(F32), gain_a[...].astype(F32).reshape(1, model_width)).astype(BF16)
    loads[0].wait()
    for item in loads[1:]:
        item.start()
    queries[me] = swap_heads(dot(normed, w_q[...]), groups, per_group).astype(BF16)
    pl.semaphore_wait(barrier, count + exp_count - 2)

    def find_slots():
        turned = table[...].T
        place = iota(turned.shape, 0) + 1
        base = me * slot_count

        def eight(n, carry):
            for i in range(8):
                hit = jnp.where(turned == base + n * 8 + i, place, 0)
                code[pl.ds(n * 8 + i, 1), :] = jnp.sum(hit, axis=0, keepdims=True)
            return carry

        lax.fori_loop(0, slot_count // 8, eight, 0)
        found = code[...]
        left = jnp.where(found > 0, lengths[...].reshape(1, requests) - (found - 1) * page, 0)
        valid[...] = jnp.broadcast_to(jnp.sum(left, axis=1, keepdims=True), valid.shape)

    def project_hidden():
        for n in range(1, 4):
            loads[n].wait()

        group = 8 if fresh % 8 == 0 else 1

        def some(n, carry):
            stored = hid[pl.ds(n * group, group)].reshape(group * page, model_width)
            place = pl.ds(kept + n * group, group)
            keys[place] = dot(stored, w_k[...]).astype(BF16).reshape(group, page, key_width)
            values[place] = dot(stored, w_v[...]).astype(BF16).reshape(group, page, key_width)
            return carry

        lax.fori_loop(0, fresh // group, some, 0)

    gather_rows(queries, me, count, q_cs, q_cr, q_ps, q_pr, find_slots, project_hidden)
    for n in range(4, 12):
        loads[n].wait()

    all_queries = queries[...].reshape(requests, width)
    chunk = 48 if slot_count % 48 == 0 else 16

    def attend(step, carry):
        take = pl.ds(pl.multiple_of(step * chunk, chunk), chunk)
        q = dot((code[take, :] > 0).astype(F32).astype(BF16), all_queries)
        sub = iota((chunk, heads, key_width), 1)
        lane_group = iota((chunk, heads, key_width), 2) >> 6
        q_rows = jnp.zeros((chunk, heads, key_width), F32)
        for p in range(per_group):
            part = q[:, p * key_width : (p + 1) * key_width]
            q_rows = jnp.where(sub - p * groups == lane_group, part[:, None, :], q_rows)
        scores = lax.dot_general(
            q_rows.astype(BF16), keys[take], (((2,), (2,)), ((0,), (0,))), preferred_element_type=F32
        ) * SCORE_SCALE
        token = iota((chunk, heads, page), 2)
        is_valid = token < valid[take, :][:, None, :]
        masked = jnp.where(is_valid, scores, NEG_FILL)
        top = jnp.max(masked, axis=-1, keepdims=True)
        weights = jnp.where(is_valid, jnp.exp(masked - top), 0.0)
        total = jnp.sum(weights, axis=-1, keepdims=True)
        mixed = lax.dot_general(
            weights.astype(BF16), values[take], (((2,), (1,)), ((0,), (0,))),
            preferred_element_type=F32,
        )
        for p in range(per_group):
            piece = jnp.where(sub - p * groups == lane_group, mixed, 0.0)
            s_out[take, p * key_width : (p + 1) * key_width] = jnp.sum(piece, axis=1)
        diag = iota((chunk, heads, LANES), 2) == iota((chunk, heads, LANES), 1)
        s_top[take, :] = jnp.sum(jnp.where(diag, top, 0.0), axis=1)
        s_sum[take, :] = jnp.sum(jnp.where(diag, total, 0.0), axis=1)
        return carry

    lax.fori_loop(0, slot_count // chunk, attend, 0)

    is_member = code[...] > 0
    hits = is_member.astype(F32).astype(BF16)
    tops = s_top[...]
    row_id = iota((LANES, requests), 0)
    top_t = jnp.zeros((LANES, requests), F32)
    for h in range(heads):
        best = jnp.max(jnp.where(is_member, tops[:, h : h + 1], NEG_FILL), axis=0, keepdims=True)
        top_t = jnp.where(row_id == h, best, top_t)
    top_t = top_t.astype(BF16)
    factor = jnp.exp(tops - dot_bt(hits, top_t))
    eye = (iota((requests, requests), 0) == iota((requests, requests), 1)).astype(F32).astype(BF16)
    local_top = dot_bt(eye, top_t)
    spread = (iota((LANES, width), 1) >> 6 == iota((LANES, width), 0)).astype(F32).astype(BF16)
    f_high, f_low = split_two(factor)
    scaled = s_out[...] * (dot(f_high, spread) + dot(f_low, spread))

    def by_request(value):
        high, low = split_two(value)
        dims = (((0,), (0,)), ((), ()))
        return lax.dot_general(hits, high, dims, preferred_element_type=F32) + lax.dot_general(
            hits, low, dims, preferred_element_type=F32
        )

    msg[:, :, 0:width] = by_request(scaled).astype(BF16).reshape(count, rows, width)
    sum_high, sum_low = split_two(by_request(s_sum[...] * factor))
    from_lane, to_lane = iota((LANES, LANES), 0), iota((LANES, LANES), 1)
    in_heads = from_lane < heads
    shift_high = (in_heads & (to_lane == from_lane + 8)).astype(F32).astype(BF16)
    shift_low = (in_heads & (to_lane == from_lane + 16)).astype(F32).astype(BF16)
    stats = local_top + dot(sum_high, shift_high) + dot(sum_low, shift_low)
    msg[:, :, width : width + LANES] = stats.astype(BF16).reshape(count, rows, LANES)

    exchange(msg, parts, me, count, a_s, a_r)
    stats = parts[:, :, width : width + LANES].reshape(count * rows, LANES)
    lane, head = iota((LANES, width), 0), iota((LANES, width), 1) >> 6
    pick_top = (lane == head).astype(F32).astype(BF16)
    pick_sum = ((lane == head + 8) | (lane == head + 16)).astype(F32).astype(BF16)
    tops = dot(stats, pick_top).reshape(count, rows, width)
    sums = dot(stats, pick_sum).reshape(count, rows, width)
    best = jnp.max(tops, axis=0)
    factor = jnp.exp(tops - best[None])
    total = jnp.sum(factor * sums, axis=0)
    accum = jnp.sum(factor * parts[:, :, 0:width].astype(F32), axis=0)
    attended = swap_heads(accum / total, per_group, groups).astype(BF16)

    for n in range(12, 16):
        loads[n].wait()
    proj_out[...] = dot(attended, w_o[...]).astype(BF16)

    def to_exp(j):
        there = lax.rem(col + j, exp_count)
        return push(proj_out, proj_in.at[j], p_s.at[j], p_r.at[j], {"exp": there})

    for j in range(1, exp_count):
        to_exp(j).start()
    for j in range(1, exp_count):
        to_exp(j).wait()
    projected = proj_out[...].astype(F32)
    for j in range(1, exp_count):
        projected = projected + proj_in[j].astype(F32)
    mixed = tok[...].astype(F32) + projected
    mixed_buf[...] = mixed
    chips = count // 2
    chip, core = me // 2, lax.rem(me, 2)
    partner = chip * 2 + (1 - core)
    rows_in[core] = rms_scale(
        mixed, gain_m[...].astype(F32).reshape(1, model_width)
    ).astype(BF16)

    def to_chip(k):
        there = lax.rem(chip + k, chips) * 2 + core
        return push(
            rows_in.at[core], rows_in.at[k * 2 + core], chip_s.at[k], chip_r.at[k], {"pool": there}
        )

    def to_core(k):
        held = rows_in.at[k * 2 + core]
        return push(held, held, core_s.at[k], core_r.at[k], {"pool": partner})

    def start_chip(k, carry):
        to_chip(k).start()
        return carry

    lax.fori_loop(1, chips, start_chip, 0)
    to_core(0).start()

    half = out.shape[1]
    cols = pl.ds(pl.multiple_of(col * half, half), half)

    def give(i):
        k, there_core = i // 2, lax.rem(i, 2)
        there = lax.rem(chip - k + chips, chips) * 2 + there_core
        return push(
            made.at[i], back.at[me], b_s.at[i], b_r.at[k * 2 + core], {"pool": there}
        )

    def forward(k, carry):
        to_chip(k).wait_recv()
        to_core(k).start()
        return carry

    def finish_core(k, carry):
        to_core(k).wait_recv()
        return carry

    def start_give(i, carry):
        give(i).start()
        return carry

    near = chips // 2
    for low, high in ((0, near), (near, chips)):
        lax.fori_loop(max(low, 1), high, forward, 0)
        lax.fori_loop(low, high, finish_core, 0)
        some = rows_in[2 * low : 2 * high].reshape((high - low) * 2 * rows, model_width)
        gate_act = dot(some, w_g[...])
        up_act = dot(some, w_u[...])
        hidden = (gate_act / (1.0 + jnp.exp(-gate_act)) * up_act).astype(BF16)
        result = dot(hidden, w_d[:, cols]).astype(BF16)
        made[2 * low : 2 * high] = result.reshape((high - low) * 2, rows, half)
        if low == 0:
            give(1 - core).start()
        lax.fori_loop(2 * max(low, 1), 2 * high, start_give, 0)

    eye_rows = iota((rows, rows), 0) == iota((rows, rows), 1)

    def weigh(e, carry):
        line = jnp.sum(jnp.where(ids[...] == e, gates[...], 0.0), axis=0, keepdims=True)
        column = jnp.sum(jnp.where(eye_rows, line, 0.0), axis=1, keepdims=True)
        coeff[e] = jnp.broadcast_to(column, (rows, LANES))
        return carry

    lax.fori_loop(0, count, weigh, 0)

    def arrival(j):
        k, from_core = j // 2, lax.rem(j, 2)
        source = lax.rem(chip + k, chips) * 2 + from_core
        return source, push(
            made.at[0], back.at[source], b_s.at[j], b_r.at[j], {"pool": partner}
        )

    own = made[core].astype(F32) * coeff[me][:, 0:1]
    total = mixed_buf[:, cols] + own
    _, first = arrival(1 - core)
    first.wait_recv()
    total = total + coeff[partner][:, 0:1] * back[partner].astype(F32)

    def combine(j, total):
        source, copy = arrival(j)
        copy.wait_recv()
        return total + coeff[source][:, 0:1] * back[source].astype(F32)

    out[...] = lax.fori_loop(2, count, combine, total).astype(BF16)

    def drain_give(i, carry):
        give(i).wait_send()
        return carry

    def drain_chip(k, carry):
        to_chip(k).wait_send()
        return carry

    def drain_core(k, carry):
        to_core(k).wait_send()
        return carry

    give(1 - core).wait_send()
    lax.fori_loop(2, count, drain_give, 0)
    lax.fori_loop(1, chips, drain_chip, 0)
    lax.fori_loop(0, chips, drain_core, 0)


def on_device(
    tokens, block_table, lengths, k_cache, v_cache, hidden_store, norm_attn, w_query, w_key, w_value,
    w_out, norm_moe, expert_ids, gate_weights, w_gate, w_up, w_down,
):
    count = lax.axis_size("pool")
    exp_count = lax.axis_size("exp")
    rows, model_width = tokens.shape
    width = w_query.shape[1]
    key_width = w_key.shape[1]
    groups = key_width // HEAD_SIZE
    per_group = width // key_width
    chips = count // 2
    dma = pltpu.SemaphoreType.DMA
    page = k_cache.shape[1]
    slot_count = k_cache.shape[0] + hidden_store.shape[0]
    requests = block_table.shape[0]
    half = model_width // exp_count
    hidden_units = w_gate.shape[2]
    big = pl.BlockSpec(memory_space=pl.ANY)
    return pl.pallas_call(
        functools.partial(layer_kernel, count, exp_count, groups, per_group),
        out_shape=jax.ShapeDtypeStruct((rows, half), BF16),
        in_specs=[VMEM] * 7 + [big] * 10,
        out_specs=VMEM,
        scratch_shapes=[
            pltpu.VMEM(w_query.shape, BF16),
            pltpu.VMEM(w_key.shape, BF16),
            pltpu.VMEM(w_value.shape, BF16),
            pltpu.VMEM(hidden_store.shape, BF16),
            pltpu.VMEM((slot_count, page, key_width), BF16),
            pltpu.VMEM((slot_count, page, key_width), BF16),
            pltpu.VMEM(w_out.shape, BF16),
            pltpu.VMEM((model_width, hidden_units), BF16),
            pltpu.VMEM((model_width, hidden_units), BF16),
            pltpu.VMEM((hidden_units, model_width), BF16),
            pltpu.VMEM((count, rows, width), BF16),
            pltpu.VMEM((slot_count, requests), jnp.int32),
            pltpu.VMEM((slot_count, page), jnp.int32),
            pltpu.VMEM((slot_count, width), F32),
            pltpu.VMEM((slot_count, LANES), F32),
            pltpu.VMEM((slot_count, LANES), F32),
            pltpu.VMEM((count, rows, width + LANES), BF16),
            pltpu.VMEM((count, rows, width + LANES), BF16),
            pltpu.VMEM((rows, model_width), BF16),
            pltpu.VMEM((exp_count, rows, model_width), BF16),
            pltpu.VMEM((count, rows, model_width), BF16),
            pltpu.VMEM((rows, model_width), F32),
            pltpu.VMEM((count, rows, half), BF16),
            pltpu.VMEM((count, rows, half), BF16),
            pltpu.VMEM((count, rows, LANES), F32),
            dma((16,)),
            dma((chips,)), dma((chips,)), dma((chips,)), dma((chips,)),
            dma((count,)), dma((count,)),
            dma((exp_count,)), dma((exp_count,)),
            dma((chips,)), dma((chips,)), dma((chips,)), dma((chips,)),
            dma((count,)), dma((count,)),
        ],
        compiler_params=pltpu.CompilerParams(
            collective_id=0, has_side_effects=True, vmem_limit_bytes=VMEM_LIMIT
        ),
        name="layer",
    )(
        tokens, norm_attn, norm_moe, block_table, lengths,
        expert_ids.T, gate_weights.T, w_query, w_key, w_value, hidden_store, k_cache, v_cache,
        w_out, w_gate[0], w_up[0], w_down[0],
    )


def solution(mesh):
    placed = (
        P("pool", None),
        P(),
        P(),
        P("pool", None, "exp"),
        P("pool", None, "exp"),
        P("pool", None, None),
        P(),
        P(None, "exp"),
        P(None, "exp"),
        P(None, "exp"),
        P("exp", None),
        P(),
        P("pool", None),
        P("pool", None),
        P("pool", None, None),
        P("pool", None, None),
        P("pool", None, None),
    )
    return jax.shard_map(
        on_device, mesh=mesh, in_specs=placed, out_specs=P("pool", "exp"), check_vma=False
    )
```
